32 devices in a mesh: seq: 8 (over y, x, core), dp: 4 (over z).
Axes of the slice: x: 2, y: 2, z: 4, core: 2. Of those that a mesh axis runs over, the one named last changes fastest.
Arguments:
- queries: bfloat16 [4, 4096, 2048], P('dp', 'seq'), may hold values from -5 to 5
- keys: bfloat16 [4, 4096, 2048], P('dp', 'seq'), may hold values from -5 to 5
- values: bfloat16 [4, 4096, 2048], P('dp', 'seq'), may hold values from -8 to 8
- out_weight: bfloat16 [2048, 4096], P(None, 'dp'), may hold values from -0.125 to 0.125
Outputs:
- projected: bfloat16 [4, 4096, 4096], P('dp', 'seq')
The draws below stay inside these ranges and needn't reach their ends.
All inputs are finite; a program needn't handle non-finite values.
Results may differ from the reference program's by a relative error of at most 0.0061.
Values may be sent and summed in bfloat16 or wider, within the bound.
A program may use at most 192 MiB of HBM per device.

```python
import math
import jax
import jax.numpy as jnp
from jax import lax

D = 4096
HEADS = 16
CHANNEL_WIDTH = 128
SEGMENT_LENGTH = 256
LENGTH = 4096
NBLK = 16
SEQS = 4


def block_offsets(key, spread):
    offsets = jax.random.uniform(key, (SEQS, NBLK, 1, HEADS * CHANNEL_WIDTH), minval=-spread, maxval=spread)
    return jnp.broadcast_to(offsets, (SEQS, NBLK, SEGMENT_LENGTH, HEADS * CHANNEL_WIDTH)).reshape(SEQS, LENGTH, HEADS * CHANNEL_WIDTH)


def draw_queries(key, part):
    main_key = jax.random.fold_in(key, 11)
    shape = (SEQS, LENGTH, HEADS * CHANNEL_WIDTH)
    drawn = jnp.clip(jax.random.normal(main_key, shape), -4.5, 4.5)
    return drawn.astype(jnp.bfloat16)


def draw_keys(key, part):
    main_key = jax.random.fold_in(key, 22)
    offset_key = jax.random.fold_in(key, 23)
    shape = (SEQS, LENGTH, HEADS * CHANNEL_WIDTH)
    drawn = jax.random.normal(main_key, shape) + block_offsets(offset_key, 1.0)
    drawn = jnp.clip(drawn, -5.0, 5.0)
    return drawn.astype(jnp.bfloat16)


def draw_values(key, part):
    main_key = jax.random.fold_in(key, 33)
    offset_key = jax.random.fold_in(key, 34)
    shape = (SEQS, LENGTH, HEADS * CHANNEL_WIDTH)
    drawn = jnp.clip(jax.random.normal(main_key, shape), -4.0, 4.0) + block_offsets(offset_key, 2.0)
    return jnp.clip(drawn, -8.0, 8.0).astype(jnp.bfloat16)


def block_levels(rng, shape, pieces, low, high):
    gain = 1.0
    for dim, shards_of in pieces:
        draws = jax.random.uniform(jax.random.fold_in(jax.random.fold_in(rng, 6), dim), (shards_of,), jnp.float32, low / len(pieces), high / len(pieces))
        gain = gain * jnp.repeat(jnp.exp(draws), shape[dim] // shards_of).reshape((-1,) + (1,) * (len(shape) - 1 - dim))
    return gain


def scatter_about(stream_key, shape, width, bound, shards=(), held_as=jnp.bfloat16):
    level = block_levels(stream_key, shape, shards, -0.22, 0.18) if shards else 1.0
    values = jax.random.normal(stream_key, shape, jnp.float32) * width * level
    return jnp.minimum(jnp.maximum(values, -bound), bound).astype(held_as)


def setup_inputs(seed: int = 0) -> dict:
    splits = jax.random.split(jax.random.key(seed), 5)
    return {
        "queries": draw_queries(jax.random.fold_in(splits[4], 71), 0),
        "keys": draw_keys(jax.random.fold_in(splits[4], 71), 0),
        "values": draw_values(jax.random.fold_in(splits[4], 71), 0),
        "out_weight": scatter_about(splits[3], (HEADS * CHANNEL_WIDTH, D), (HEADS * CHANNEL_WIDTH) ** -0.5, 0.125, ((1, 4),)),
    }


def reference(queries, keys, values, out_weight):
    feature_width = HEADS * CHANNEL_WIDTH
    softmax_multiplier = 1.0 / math.sqrt(CHANNEL_WIDTH)
    faraway_offset_bias = math.log(SEGMENT_LENGTH)

    def block_means(tensor):
        summed = lax.optimization_barrier(jnp.mean(tensor.astype(jnp.float32).reshape(SEQS, NBLK, SEGMENT_LENGTH, feature_width), axis=2))
        rounded = lax.optimization_barrier(summed.astype(jnp.bfloat16))
        return rounded.astype(jnp.float32).reshape(SEQS, NBLK, HEADS, CHANNEL_WIDTH)
    span_address_means = block_means(keys)
    value_means = block_means(values)
    padding = jnp.zeros((SEQS, SEGMENT_LENGTH, feature_width), keys.dtype)
    keys_padded = jnp.concatenate([padding, keys], axis=1)
    values_padded = jnp.concatenate([padding, values], axis=1)
    query_pos = jnp.arange(SEGMENT_LENGTH, dtype=jnp.int32)
    key_pos = jnp.arange(2 * SEGMENT_LENGTH, dtype=jnp.int32)
    far_index = jnp.arange(NBLK, dtype=jnp.int32)

    def one_block(block_id):
        first_row = (block_id * SEGMENT_LENGTH).astype(jnp.int32)
        request_vectors = lax.dynamic_slice_in_dim(queries, first_row, SEGMENT_LENGTH, 1).astype(jnp.float32).reshape(SEQS, SEGMENT_LENGTH, HEADS, CHANNEL_WIDTH)
        address_vectors = lax.dynamic_slice_in_dim(keys_padded, first_row, 2 * SEGMENT_LENGTH, 1).astype(jnp.float32).reshape(SEQS, 2 * SEGMENT_LENGTH, HEADS, CHANNEL_WIDTH)
        value_rows = lax.dynamic_slice_in_dim(values_padded, first_row, 2 * SEGMENT_LENGTH, 1).astype(jnp.float32).reshape(SEQS, 2 * SEGMENT_LENGTH, HEADS, CHANNEL_WIDTH)
        adjacent_similarity = jnp.einsum('zplr,zblr->zlpb', request_vectors, address_vectors) * softmax_multiplier
        within_block = (key_pos[None, :] >= SEGMENT_LENGTH) & (key_pos[None, :] - SEGMENT_LENGTH <= query_pos[:, None])
        preceding_segment = (key_pos[None, :] < SEGMENT_LENGTH) & (block_id >= 1)
        adjacent_similarity = jnp.where((within_block | preceding_segment)[None, None], adjacent_similarity, -jnp.inf)
        faraway_similarity = jnp.einsum('fwqo,fxqo->fqwx', request_vectors, span_address_means) * softmax_multiplier + faraway_offset_bias
        faraway_similarity = jnp.where((far_index < block_id - 1)[None, None, None, :], faraway_similarity, -jnp.inf)
        row_max = jnp.maximum(lax.optimization_barrier(jnp.max(adjacent_similarity, axis=-1)), lax.optimization_barrier(jnp.max(faraway_similarity, axis=-1)))[..., None]
        near_w = jnp.exp(adjacent_similarity - row_max)
        far_w = jnp.exp(faraway_similarity - row_max)
        row_total = lax.optimization_barrier(jnp.sum(near_w, axis=-1, keepdims=True)) + lax.optimization_barrier(jnp.sum(far_w, axis=-1, keepdims=True))
        near_p = lax.optimization_barrier((near_w / row_total).astype(jnp.bfloat16)).astype(jnp.float32)
        far_p = lax.optimization_barrier((far_w / row_total).astype(jnp.bfloat16)).astype(jnp.float32)
        attended = jnp.einsum('shqk,skhd->sqhd', near_p, value_rows) + jnp.einsum('shqj,sjhd->sqhd', far_p, value_means)
        attended = attended.astype(jnp.bfloat16).reshape(SEQS * SEGMENT_LENGTH, feature_width)
        result = jnp.dot(attended, out_weight, preferred_element_type=jnp.float32).astype(jnp.bfloat16)
        return result.reshape(SEQS, SEGMENT_LENGTH, D)
    segment_outcomes = lax.map(one_block, jnp.arange(NBLK, dtype=jnp.int32))
    return jnp.transpose(segment_outcomes, (1, 0, 2, 3)).reshape(SEQS, LENGTH, D)
```

```python
import functools
import math

import jax
import jax.numpy as jnp
from jax import lax
from jax.experimental import pallas as pl
from jax.experimental.pallas import tpu as pltpu
from jax.sharding import PartitionSpec as P

CHANNEL_WIDTH = 128
SEGMENT_LENGTH = 256
MESH = pl.DeviceIdType.MESH
MEAN_ROWS = 8


def nearest_first(position, count):
    return sorted((e for e in range(count) if e != position), key=lambda e: (abs(e - position), e))


def fused(
    n, m, q_hbm, k_hbm, v_hbm, w_hbm, out_hbm,
    q_buf, k_buf, v_buf, w_buf, att, means, far_k, far_v, stage,
    load_sem, halo_send, halo_recv, mean_send, mean_recv,
    z_send, w_send, w_recv, out_sem,
):
    rows, feature = q_hbm.shape
    cols = w_hbm.shape[1]
    heads = feature // CHANNEL_WIDTH
    seg = SEGMENT_LENGTH
    local_blocks = rows // seg
    chunks = MEAN_ROWS // local_blocks
    chunk_width = feature // chunks
    chunk_heads = heads // chunks
    piece = feature // n
    p = lax.axis_index("seq")
    d = lax.axis_index("dp")

    barrier = pltpu.get_barrier_semaphore()

    def greet(i, carry):
        pl.semaphore_signal(barrier, inc=1, device_id=(lax.rem(p + i, n), d), device_id_type=MESH)
        return carry

    lax.fori_loop(1, n, greet, 0)

    @pl.when(d > 0)
    def _():
        pl.semaphore_signal(barrier, inc=1, device_id=(p, d - 1), device_id_type=MESH)

    @pl.when(d < m - 1)
    def _():
        pl.semaphore_signal(barrier, inc=1, device_id=(p, d + 1), device_id_type=MESH)

    load_k = pltpu.make_async_copy(k_hbm, k_buf.at[pl.ds(seg, rows)], load_sem.at[0])
    load_v = pltpu.make_async_copy(v_hbm, v_buf.at[pl.ds(seg, rows)], load_sem.at[1])
    load_q = pltpu.make_async_copy(q_hbm, q_buf, load_sem.at[2])
    load_w = pltpu.make_async_copy(w_hbm, w_buf.at[d], load_sem.at[3])
    for load in (load_k, load_v, load_q, load_w):
        load.start()

    @pl.when(p == 0)
    def _():
        k_buf[0:seg, :] = jnp.zeros((seg, feature), k_buf.dtype)
        v_buf[0:seg, :] = jnp.zeros((seg, feature), v_buf.dtype)

    far_k[...] = jnp.zeros_like(far_k)
    far_v[...] = jnp.zeros_like(far_v)

    z_count = jnp.where(d > 0, 1, 0) + jnp.where(d < m - 1, 1, 0)
    pl.semaphore_wait(barrier, n - 1 + z_count)

    last = pl.ds(rows - seg, seg)
    halo = [
        pltpu.make_async_remote_copy(
            src_ref=src.at[last], dst_ref=dst.at[pl.ds(0, seg)],
            send_sem=halo_send.at[i], recv_sem=halo_recv.at[i],
            device_id=(lax.rem(p + 1, n), d), device_id_type=MESH,
        )
        for i, (src, dst) in enumerate(((k_hbm, k_buf), (v_hbm, v_buf)))
    ]

    my_rows = pl.ds(pl.multiple_of(p * piece, piece), piece)

    def z_own(side, target):
        return pltpu.make_async_remote_copy(
            src_ref=w_hbm.at[my_rows], dst_ref=w_buf.at[d, my_rows],
            send_sem=z_send.at[side], recv_sem=w_recv.at[d, p],
            device_id=(p, target), device_id_type=MESH,
        )

    @pl.when(d > 0)
    def _():
        z_own(0, d - 1).start()

    @pl.when(d < m - 1)
    def _():
        z_own(1, d + 1).start()

    @pl.when(p < n - 1)
    def _():
        for copy in halo:
            copy.start()

    tables = [nearest_first(e, m) for e in range(m)]
    sources = []
    for j in range(m - 1):
        e = 0
        for at in range(m):
            e = e + jnp.where(d == at, tables[at][j], 0)
        sources.append(e)
    bits = []
    b = 2
    while b < n:
        bits.append(b)
        b *= 2
    core = lax.rem(p, 2)
    flips = [bit * (1 - 2 * lax.rem(p // bit, 2)) for bit in bits]
    hops = [flips[s] + core * (flips[-1 - s] - flips[s]) for s in range(len(bits))]
    hops.append(1 - 2 * core)
    stages = len(hops)

    def w_rows(r):
        return pl.ds(pl.multiple_of(r * piece, piece), piece)

    def w_copy(j, slot, r, target):
        ref = w_buf.at[sources[j], w_rows(r)]
        return pltpu.make_async_remote_copy(
            src_ref=ref, dst_ref=ref,
            send_sem=w_send.at[j, slot], recv_sem=w_recv.at[sources[j], r],
            device_id=target, device_id_type=MESH,
        )

    def arrivals(s):
        if s == 0:
            return [p]
        held = [p]
        for hop in hops[: s - 1]:
            held = held + [r + hop for r in held]
        return [r + hops[s - 1] for r in held]

    sent = []

    def serve(j, s):
        e = sources[j]
        for at, r in enumerate(arrivals(s)):
            w_copy(j, 0, r, (p, d)).wait_recv()
            if s == 0:
                onward = jnp.where(e < d, d + 1, d - 1)

                @pl.when(jnp.logical_and(onward >= 0, onward < m))
                def _():
                    pltpu.make_async_remote_copy(
                        src_ref=w_buf.at[e, my_rows], dst_ref=w_buf.at[e, my_rows],
                        send_sem=z_send.at[2 + j], recv_sem=w_recv.at[e, p],
                        device_id=(p, onward), device_id_type=MESH,
                    ).start()
            for later in range(s, stages):
                slot = len([1 for x in sent if x[0] == j])
                copy = w_copy(j, slot, r, (p + hops[later], d))
                copy.start()
                sent.append((j, copy))

    load_k.wait()
    load_v.wait()
    ones = jnp.ones((MEAN_ROWS, seg), jnp.bfloat16)
    row_index = lax.broadcasted_iota(jnp.int32, (MEAN_ROWS, chunk_width), 0)
    packed = []
    for buf in (k_buf, v_buf):
        part = jnp.zeros((MEAN_ROWS, chunk_width), jnp.float32)
        for i in range(local_blocks):
            for c in range(chunks):
                block = buf[seg * (i + 1) : seg * (i + 2), c * chunk_width : (c + 1) * chunk_width]
                total = jnp.dot(ones, block, preferred_element_type=jnp.float32)
                part = jnp.where(row_index == c * local_blocks + i, total * (1.0 / seg), part)
        packed.append(part)
    means[p] = jnp.concatenate(packed, axis=0).astype(means.dtype)

    def mean_copy(i, source):
        return pltpu.make_async_remote_copy(
            src_ref=means.at[source], dst_ref=means.at[source],
            send_sem=mean_send.at[i], recv_sem=mean_recv.at[source],
            device_id=(lax.rem(p + i, n), d), device_id_type=MESH,
        )

    def send_mean(i, carry):
        mean_copy(i, p).start()
        return carry

    lax.fori_loop(1, n - p, send_mean, 0)

    def unpack(at, carry):
        @pl.when(at < p)
        def _():
            mean_copy(1, at).wait_recv()

        both = means[at].astype(jnp.float32)
        to = pl.ds(pl.multiple_of(at * MEAN_ROWS, MEAN_ROWS), MEAN_ROWS)
        far_k[to, :] = both[:MEAN_ROWS]
        far_v[to, :] = both[MEAN_ROWS:]
        return carry

    load_q.wait()
    lax.fori_loop(0, p + 1, unpack, 0)

    scale = math.log2(math.e) / math.sqrt(CHANNEL_WIDTH)
    far_bias = math.log2(seg)
    contract = (((1,), (1,)), ((), ()))

    def head(i, h):
        lanes = pl.ds(pl.multiple_of(h * CHANNEL_WIDTH, CHANNEL_WIDTH), CHANNEL_WIDTH)
        q = q_buf[seg * i : seg * (i + 1), lanes]
        chunk = h // chunk_heads
        within = pl.ds(pl.multiple_of(lax.rem(h, chunk_heads) * CHANNEL_WIDTH, CHANNEL_WIDTH), CHANNEL_WIDTH)
        fk = far_k[:, within].astype(jnp.bfloat16)
        fv = far_v[:, within].astype(jnp.bfloat16)
        before = lax.dot_general(q, k_buf[seg * i : seg * (i + 1), lanes], contract, preferred_element_type=jnp.float32) * scale
        inside = lax.dot_general(q, k_buf[seg * (i + 1) : seg * (i + 2), lanes], contract, preferred_element_type=jnp.float32) * scale
        far = lax.dot_general(q, fk, contract, preferred_element_type=jnp.float32) * scale
        if i == 0:
            before = before + jnp.where(p == 0, -jnp.inf, 0.0)
        q_at = lax.broadcasted_iota(jnp.int32, (seg, seg), 0)
        k_at = lax.broadcasted_iota(jnp.int32, (seg, seg), 1)
        inside = jnp.where(k_at <= q_at, inside, -jnp.inf)
        slot = lax.broadcasted_iota(jnp.int32, (1, n * MEAN_ROWS), 1)
        in_tile = lax.rem(slot, MEAN_ROWS)
        block = (slot // MEAN_ROWS) * local_blocks + lax.rem(in_tile, local_blocks)
        usable = jnp.logical_and(in_tile // local_blocks == chunk, block < p * local_blocks + i - 1)
        far = far + jnp.where(usable, far_bias, -jnp.inf)
        top = jnp.maximum(
            jnp.max(jnp.maximum(before, inside), axis=1, keepdims=True),
            jnp.max(far, axis=1, keepdims=True),
        )
        before = jnp.exp2(before - top)
        inside = jnp.exp2(inside - top)
        far = jnp.exp2(far - top)
        total = jnp.sum(before + inside, axis=1, keepdims=True) + jnp.sum(far, axis=1, keepdims=True)
        mixed = jnp.dot(before.astype(jnp.bfloat16), v_buf[seg * i : seg * (i + 1), lanes], preferred_element_type=jnp.float32)
        mixed += jnp.dot(inside.astype(jnp.bfloat16), v_buf[seg * (i + 1) : seg * (i + 2), lanes], preferred_element_type=jnp.float32)
        mixed += jnp.dot(far.astype(jnp.bfloat16), fv, preferred_element_type=jnp.float32)
        att[seg * i : seg * (i + 1), lanes] = (mixed / total).astype(att.dtype)

    def attend(i):
        def pair(g, carry):
            head(i, 2 * g)
            head(i, 2 * g + 1)
            return carry

        lax.fori_loop(0, heads // 2, pair, 0)

    tile = min(256, cols)

    def out_copy(slot, e):
        to = pl.ds(pl.multiple_of(e * cols, cols), cols)
        return pltpu.make_async_copy(stage.at[slot], out_hbm.at[:, to], out_sem.at[slot])

    def project(count, e):
        slot = count % 2
        if count >= 2:
            out_copy(slot, e).wait()

        def one(t, carry):
            lanes = pl.ds(pl.multiple_of(t * tile, tile), tile)
            stage[slot, :, lanes] = jnp.dot(
                att[...], w_buf[e, :, lanes], preferred_element_type=jnp.float32
            ).astype(stage.dtype)
            return carry

        lax.fori_loop(0, cols // tile, one, 0)
        out_copy(slot, e).start()

    order = sorted(
        ((j, s) for j in range(m - 1) for s in range(stages + 1)), key=lambda js: (2 * js[0] + js[1], js[1])
    )
    due = list(order)

    def serve_next(count):
        for _ in range(min(count, len(due))):
            serve(*due.pop(0))

    for i in range(1, local_blocks):
        attend(i)
    serve_next(2)

    @pl.when(p > 0)
    def _():
        for copy in halo:
            copy.wait_recv()

    attend(0)
    load_w.wait()
    serve_next(2)
    project(0, d)
    done = 0
    while due:
        j, s = due[0]
        serve_next(1)
        if s == stages:
            done += 1
            project(done, sources[j])

    for count in range(max(0, m - 2), m):
        out_copy(count % 2, d).wait()

    @pl.when(d > 0)
    def _():
        z_own(0, d - 1).wait_send()

    @pl.when(d < m - 1)
    def _():
        z_own(1, d + 1).wait_send()

    for j in range(m - 1):
        e = sources[j]
        onward = jnp.where(e < d, d + 1, d - 1)

        @pl.when(jnp.logical_and(onward >= 0, onward < m))
        def _():
            pltpu.make_async_remote_copy(
                src_ref=w_buf.at[e, my_rows], dst_ref=w_buf.at[e, my_rows],
                send_sem=z_send.at[2 + j], recv_sem=w_recv.at[e, p],
                device_id=(p, onward), device_id_type=MESH,
            ).wait_send()

    for _, copy in sent:
        copy.wait_send()

    @pl.when(p < n - 1)
    def _():
        for copy in halo:
            copy.wait_send()

    def mean_sent(i, carry):
        mean_copy(i, p).wait_send()
        return carry

    lax.fori_loop(1, n - p, mean_sent, 0)


def per_device(n, m, queries, keys, values, out_weight):
    rows, feature = queries.shape[1:]
    cols = out_weight.shape[1]
    local_blocks = rows // SEGMENT_LENGTH
    chunk_width = feature * local_blocks // MEAN_ROWS
    bf16 = jnp.bfloat16
    out = pl.pallas_call(
        functools.partial(fused, n, m),
        out_shape=jax.ShapeDtypeStruct((rows, m * cols), bf16),
        in_specs=[pl.BlockSpec(memory_space=pl.ANY)] * 4,
        out_specs=pl.BlockSpec(memory_space=pl.ANY),
        scratch_shapes=[
            pltpu.VMEM((rows, feature), bf16),
            pltpu.VMEM((rows + SEGMENT_LENGTH, feature), bf16),
            pltpu.VMEM((rows + SEGMENT_LENGTH, feature), bf16),
            pltpu.VMEM((m, feature, cols), bf16),
            pltpu.VMEM((rows, feature), bf16),
            pltpu.VMEM((n, 2 * MEAN_ROWS, chunk_width), bf16),
            pltpu.VMEM((n * MEAN_ROWS, chunk_width), jnp.float32),
            pltpu.VMEM((n * MEAN_ROWS, chunk_width), jnp.float32),
            pltpu.VMEM((2, rows, cols), bf16),
            pltpu.SemaphoreType.DMA((4,)),
            pltpu.SemaphoreType.DMA((2,)),
            pltpu.SemaphoreType.DMA((2,)),
            pltpu.SemaphoreType.DMA((n,)),
            pltpu.SemaphoreType.DMA((n,)),
            pltpu.SemaphoreType.DMA((m + 1,)),
            pltpu.SemaphoreType.DMA((m - 1, n - 1)),
            pltpu.SemaphoreType.DMA((m, n)),
            pltpu.SemaphoreType.DMA((2,)),
        ],
        compiler_params=pltpu.CompilerParams(
            collective_id=0, has_side_effects=True, vmem_limit_bytes=56 * 1024 * 1024
        ),
    )(queries[0], keys[0], values[0], out_weight)
    return out[None]


def solution(mesh):
    return jax.shard_map(
        functools.partial(per_device, mesh.shape["seq"], mesh.shape["dp"]),
        mesh=mesh,
        in_specs=(P("dp", "seq", None), P("dp", "seq", None), P("dp", "seq", None), P(None, "dp")),
        out_specs=P("dp", "seq", None),
        check_vma=False,
    )
```

```python
import functools
import math

import jax
import jax.numpy as jnp
from jax import lax
from jax.experimental import pallas as pl
from jax.experimental.pallas import tpu as pltpu
from jax.sharding import PartitionSpec as P

CHANNEL_WIDTH = 128
SEGMENT_LENGTH = 256
MESH = pl.DeviceIdType.MESH
SUB = 1
MEAN_ROWS = 8


def nearest_first(position, count):
    return sorted((e for e in range(count) if e != position), key=lambda e: (abs(e - position), e))


def fused(
    n, m, q_hbm, k_hbm, v_hbm, w_hbm, out_hbm,
    q_buf, k_buf, v_buf, w_buf, att, means, far_k, far_v, stage,
    load_sem, halo_send, halo_recv, mean_send, mean_recv,
    z_send, w_send, w_recv, out_sem,
):
    rows, feature = q_hbm.shape
    cols = w_hbm.shape[1]
    heads = feature // CHANNEL_WIDTH
    seg = SEGMENT_LENGTH
    local_blocks = rows // seg
    chunks = MEAN_ROWS // local_blocks
    chunk_width = feature // chunks
    chunk_heads = heads // chunks
    piece = feature // (n * SUB)
    p = lax.axis_index("seq")
    d = lax.axis_index("dp")

    barrier = pltpu.get_barrier_semaphore()

    def greet(i, carry):
        pl.semaphore_signal(barrier, inc=1, device_id=(lax.rem(p + i, n), d), device_id_type=MESH)
        return carry

    lax.fori_loop(1, n, greet, 0)

    @pl.when(d > 0)
    def _():
        pl.semaphore_signal(barrier, inc=1, device_id=(p, d - 1), device_id_type=MESH)

    @pl.when(d < m - 1)
    def _():
        pl.semaphore_signal(barrier, inc=1, device_id=(p, d + 1), device_id_type=MESH)

    load_k = pltpu.make_async_copy(k_hbm, k_buf.at[pl.ds(seg, rows)], load_sem.at[0])
    load_v = pltpu.make_async_copy(v_hbm, v_buf.at[pl.ds(seg, rows)], load_sem.at[1])
    load_q = pltpu.make_async_copy(q_hbm, q_buf, load_sem.at[2])
    load_w = pltpu.make_async_copy(w_hbm, w_buf.at[d], load_sem.at[3])
    for load in (load_k, load_v, load_q, load_w):
        load.start()

    @pl.when(p == 0)
    def _():
        k_buf[0:seg, :] = jnp.zeros((seg, feature), k_buf.dtype)
        v_buf[0:seg, :] = jnp.zeros((seg, feature), v_buf.dtype)

    far_k[...] = jnp.zeros_like(far_k)
    far_v[...] = jnp.zeros_like(far_v)

    z_count = jnp.where(d > 0, 1, 0) + jnp.where(d < m - 1, 1, 0)
    pl.semaphore_wait(barrier, n - 1 + z_count)

    def halo_copy(i):
        src, dst = ((k_hbm, k_buf), (v_hbm, v_buf))[i]
        return pltpu.make_async_remote_copy(
            src_ref=src.at[pl.ds(rows - seg, seg)], dst_ref=dst.at[pl.ds(0, seg)],
            send_sem=halo_send.at[i], recv_sem=halo_recv.at[i],
            device_id=(lax.rem(p + 1, n), d), device_id_type=MESH,
        )

    tables = [nearest_first(e, m) for e in range(m)]
    sources = []
    for j in range(m - 1):
        e = 0
        for at in range(m):
            e = e + jnp.where(d == at, tables[at][j], 0)
        sources.append(e)

    bits = []
    b = 2
    while b < n:
        bits.append(b)
        b *= 2
    bits = bits[::-1]
    core = lax.rem(p, 2)
    flips = [bit * (1 - 2 * lax.rem(p // bit, 2)) for bit in bits]
    peer = 1 - 2 * core

    def plan(roots, hops):
        held, events = [], []
        for at, root in enumerate(roots):
            held.append((p + root, 1 - 2 * at))
            events.append((p + root, list(hops), True))
        for s, hop in enumerate(hops):
            new = [(r + sign * hop, sign) for r, sign in held]
            events += [(r, list(hops[s + 1 :]), False) for r, _ in new]
            held += new
        return events

    plans = (
        plan([0], flips),
        plan([0, sum(flips)], flips[:-1]) if bits else plan([0], flips),
    )

    def pick(even, odd):
        return even + core * (odd - even)

    events = []
    for even, odd in zip(*plans):
        targets = []
        for at in range(max(len(even[1]), len(odd[1]))):
            if at >= len(odd[1]):
                targets.append((0, even[1][at]))
            elif at >= len(even[1]):
                targets.append((1, odd[1][at]))
            else:
                targets.append((None, pick(even[1][at], odd[1][at])))
        targets.append((None, peer))
        root = None if even[2] and odd[2] else 0 if even[2] else 1 if odd[2] else 2
        events.append((pick(even[0], odd[0]), targets, root))
    peer_pieces = [r + peer for r, _, _ in events]
    roots = [(r, root) for r, _, root in events if root != 2]

    def on_core(which, run):
        if which is None:
            run()
        else:
            pl.when(core == which)(run)

    def w_rows(r, u):
        return pl.ds(pl.multiple_of((r * SUB + u) * piece, piece), piece)

    def z_own(at, u, side):
        r = roots[at][0]
        return pltpu.make_async_remote_copy(
            src_ref=w_hbm.at[w_rows(r, u)], dst_ref=w_buf.at[d, w_rows(r, u)],
            send_sem=z_send.at[side, at, u], recv_sem=w_recv.at[d, r, u],
            device_id=(p, d - 1 + 2 * side), device_id_type=MESH,
        )

    def each_own(act):
        for u in range(SUB):
            for at, (_, root) in enumerate(roots):
                for side in range(2):
                    has = d > 0 if side == 0 else d < m - 1
                    if root is not None:
                        has = jnp.logical_and(has, core == root)

                    @pl.when(has)
                    def _():
                        act(z_own(at, u, side))

    each_own(lambda copy: copy.start())

    @pl.when(p < n - 1)
    def _():
        halo_copy(0).start()
        halo_copy(1).start()

    def w_copy(j, u, slot, r, target):
        ref = w_buf.at[sources[j], w_rows(r, u)]
        return pltpu.make_async_remote_copy(
            src_ref=ref, dst_ref=ref,
            send_sem=w_send.at[j, u, slot], recv_sem=w_recv.at[sources[j], r, u],
            device_id=target, device_id_type=MESH,
        )

    def z_onward(j, u, at, act):
        r, root = roots[at]
        e = sources[j]
        onward = jnp.where(e < d, d + 1, d - 1)
        has = jnp.logical_and(onward >= 0, onward < m)
        if root is not None:
            has = jnp.logical_and(has, core == root)

        @pl.when(has)
        def _():
            act(pltpu.make_async_remote_copy(
                src_ref=w_buf.at[e, w_rows(r, u)], dst_ref=w_buf.at[e, w_rows(r, u)],
                send_sem=z_send.at[2 + j, at, u], recv_sem=w_recv.at[e, r, u],
                device_id=(p, onward), device_id_type=MESH,
            ))

    def serve(j, u, i):
        r, targets, root = events[i]
        w_copy(j, u, 0, r, (p, d)).wait_recv()
        if root != 2:
            z_onward(j, u, i, lambda copy: copy.start())
        for at, (which, target) in enumerate(targets):
            on_core(which, w_copy(j, u, first_slot[i] + at, r, (p + target, d)).start)

    first_slot = [sum(len(event[1]) for event in events[:i]) for i in range(len(events))]

    def each_sent(act):
        for j in range(m - 1):
            for u in range(SUB):
                for i, (r, targets, _) in enumerate(events):
                    for at, (which, target) in enumerate(targets):
                        copy = w_copy(j, u, first_slot[i] + at, r, (p + target, d))
                        on_core(which, functools.partial(act, copy))

    def finish(j):
        for u in range(SUB):
            for r in peer_pieces:
                w_copy(j, u, 0, r, (p, d)).wait_recv()

    load_k.wait()
    load_v.wait()
    ones = jnp.ones((MEAN_ROWS, seg), jnp.bfloat16)
    row_index = lax.broadcasted_iota(jnp.int32, (MEAN_ROWS, chunk_width), 0)
    packed = []
    for buf in (k_buf, v_buf):
        part = jnp.zeros((MEAN_ROWS, chunk_width), jnp.float32)
        for i in range(local_blocks):
            for c in range(chunks):
                block = buf[seg * (i + 1) : seg * (i + 2), c * chunk_width : (c + 1) * chunk_width]
                total = jnp.dot(ones, block, preferred_element_type=jnp.float32)
                part = jnp.where(row_index == c * local_blocks + i, total * (1.0 / seg), part)
        packed.append(part)
    means[p] = jnp.concatenate(packed, axis=0).astype(means.dtype)

    def mean_copy(i, source):
        return pltpu.make_async_remote_copy(
            src_ref=means.at[source], dst_ref=means.at[source],
            send_sem=mean_send.at[i], recv_sem=mean_recv.at[source],
            device_id=(lax.rem(p + i, n), d), device_id_type=MESH,
        )

    def send_mean(i, carry):
        mean_copy(i, p).start()
        return carry

    lax.fori_loop(1, n - p, send_mean, 0)

    def unpack(at, carry):
        @pl.when(at < p)
        def _():
            mean_copy(1, at).wait_recv()

        both = means[at].astype(jnp.float32)
        to = pl.ds(pl.multiple_of(at * MEAN_ROWS, MEAN_ROWS), MEAN_ROWS)
        far_k[to, :] = both[:MEAN_ROWS]
        far_v[to, :] = both[MEAN_ROWS:]
        return carry

    load_q.wait()
    lax.fori_loop(0, p + 1, unpack, 0)

    scale = math.log2(math.e) / math.sqrt(CHANNEL_WIDTH)
    far_bias = math.log2(seg)
    contract = (((1,), (1,)), ((), ()))

    def head(i, h):
        lanes = pl.ds(pl.multiple_of(h * CHANNEL_WIDTH, CHANNEL_WIDTH), CHANNEL_WIDTH)
        q = q_buf[seg * i : seg * (i + 1), lanes]
        chunk = h // chunk_heads
        within = pl.ds(pl.multiple_of(lax.rem(h, chunk_heads) * CHANNEL_WIDTH, CHANNEL_WIDTH), CHANNEL_WIDTH)
        fk = far_k[:, within].astype(jnp.bfloat16)
        fv = far_v[:, within].astype(jnp.bfloat16)
        before = lax.dot_general(q, k_buf[seg * i : seg * (i + 1), lanes], contract, preferred_element_type=jnp.float32) * scale
        inside = lax.dot_general(q, k_buf[seg * (i + 1) : seg * (i + 2), lanes], contract, preferred_element_type=jnp.float32) * scale
        far = lax.dot_general(q, fk, contract, preferred_element_type=jnp.float32) * scale
        if i == 0:
            before = before + jnp.where(p == 0, -jnp.inf, 0.0)
        q_at = lax.broadcasted_iota(jnp.int32, (seg, seg), 0)
        k_at = lax.broadcasted_iota(jnp.int32, (seg, seg), 1)
        inside = jnp.where(k_at <= q_at, inside, -jnp.inf)
        slot = lax.broadcasted_iota(jnp.int32, (1, n * MEAN_ROWS), 1)
        in_tile = lax.rem(slot, MEAN_ROWS)
        block = (slot // MEAN_ROWS) * local_blocks + lax.rem(in_tile, local_blocks)
        usable = jnp.logical_and(in_tile // local_blocks == chunk, block < p * local_blocks + i - 1)
        far = far + jnp.where(usable, far_bias, -jnp.inf)
        top = jnp.maximum(
            jnp.max(jnp.maximum(before, inside), axis=1, keepdims=True),
            jnp.max(far, axis=1, keepdims=True),
        )
        before = jnp.exp2(before - top)
        inside = jnp.exp2(inside - top)
        far = jnp.exp2(far - top)
        total = jnp.sum(before + inside, axis=1, keepdims=True) + jnp.sum(far, axis=1, keepdims=True)
        mixed = jnp.dot(before.astype(jnp.bfloat16), v_buf[seg * i : seg * (i + 1), lanes], preferred_element_type=jnp.float32)
        mixed += jnp.dot(inside.astype(jnp.bfloat16), v_buf[seg * (i + 1) : seg * (i + 2), lanes], preferred_element_type=jnp.float32)
        mixed += jnp.dot(far.astype(jnp.bfloat16), fv, preferred_element_type=jnp.float32)
        att[seg * i : seg * (i + 1), lanes] = (mixed / total).astype(att.dtype)

    def attend(i, part, parts):
        def pair(g, carry):
            head(i, 2 * g)
            head(i, 2 * g + 1)
            return carry

        count = heads // 2 // parts
        lax.fori_loop(part * count, (part + 1) * count, pair, 0)

    tile = min(256, cols)

    def out_copy(slot, e):
        to = pl.ds(pl.multiple_of(e * cols, cols), cols)
        return pltpu.make_async_copy(stage.at[slot], out_hbm.at[:, to], out_sem.at[slot])

    def project(count, e):
        slot = count % 2
        if count >= 2:
            out_copy(slot, e).wait()

        def one(t, carry):
            lanes = pl.ds(pl.multiple_of(t * tile, tile), tile)
            stage[slot, :, lanes] = jnp.dot(
                att[...], w_buf[e, :, lanes], preferred_element_type=jnp.float32
            ).astype(stage.dtype)
            return carry

        lax.fori_loop(0, cols // tile, one, 0)
        out_copy(slot, e).start()

    def halo_here():
        @pl.when(p > 0)
        def _():
            halo_copy(0).wait_recv()
            halo_copy(1).wait_recv()

    def own_columns():
        load_w.wait()
        project(0, d)

    parts = 4
    early = [functools.partial(attend, i, part, parts) for i in range(1, local_blocks) for part in range(parts)]
    late = [functools.partial(attend, 0, part, parts) for part in range(parts)]
    half = len(early) // 2
    for run in early[:half]:
        run()
    work = {0: early[half:], 2: [halo_here] + late[:2], 3: late[2:] + [own_columns]}

    agenda = []
    for j in range(m - 1):
        for u in range(SUB):
            for i, (_, _, root) in enumerate(events):
                hops = bin(i).count("1")
                if root == 1:
                    agenda.append((j * SUB + u, j, u, i, 1))
                    agenda.append((j * SUB + u + hops, j, u, i, 0))
                else:
                    agenda.append((j * SUB + u + hops, j, u, i, None))
    agenda.sort(key=lambda entry: (entry[0], -entry[1], -entry[2], entry[3]))
    deepest = max(entry[0] for entry in agenda) - ((m - 1) * SUB - 1)
    levels = max((m - 1) * SUB + deepest, max(work) + 1)
    done = 0
    for level in range(levels):
        for due, j, u, i, which in agenda:
            if due == level:
                on_core(which, functools.partial(serve, j, u, i))
        for run in work.get(level, []):
            run()
        while level >= max(work) and done < m - 1 and (done + 1) * SUB + deepest <= level:
            finish(done)
            done += 1
            project(done, sources[done - 1])
    while done < m - 1:
        finish(done)
        done += 1
        project(done, sources[done - 1])

    for count in range(max(0, m - 2), m):
        out_copy(count % 2, d).wait()

    each_own(lambda copy: copy.wait_send())
    for j in range(m - 1):
        for u in range(SUB):
            for at in range(len(roots)):
                z_onward(j, u, at, lambda copy: copy.wait_send())
    each_sent(lambda copy: copy.wait_send())

    @pl.when(p < n - 1)
    def _():
        halo_copy(0).wait_send()
        halo_copy(1).wait_send()

    def mean_sent(i, carry):
        mean_copy(i, p).wait_send()
        return carry

    lax.fori_loop(1, n - p, mean_sent, 0)


def per_device(n, m, queries, keys, values, out_weight):
    rows, feature = queries.shape[1:]
    cols = out_weight.shape[1]
    local_blocks = rows // SEGMENT_LENGTH
    chunk_width = feature * local_blocks // MEAN_ROWS
    bf16 = jnp.bfloat16
    out = pl.pallas_call(
        functools.partial(fused, n, m),
        out_shape=jax.ShapeDtypeStruct((rows, m * cols), bf16),
        in_specs=[pl.BlockSpec(memory_space=pl.ANY)] * 4,
        out_specs=pl.BlockSpec(memory_space=pl.ANY),
        scratch_shapes=[
            pltpu.VMEM((rows, feature), bf16),
            pltpu.VMEM((rows + SEGMENT_LENGTH, feature), bf16),
            pltpu.VMEM((rows + SEGMENT_LENGTH, feature), bf16),
            pltpu.VMEM((m, feature, cols), bf16),
            pltpu.VMEM((rows, feature), bf16),
            pltpu.VMEM((n, 2 * MEAN_ROWS, chunk_width), bf16),
            pltpu.VMEM((n * MEAN_ROWS, chunk_width), jnp.float32),
            pltpu.VMEM((n * MEAN_ROWS, chunk_width), jnp.float32),
            pltpu.VMEM((2, rows, cols), bf16),
            pltpu.SemaphoreType.DMA((4,)),
            pltpu.SemaphoreType.DMA((2,)),
            pltpu.SemaphoreType.DMA((2,)),
            pltpu.SemaphoreType.DMA((n,)),
            pltpu.SemaphoreType.DMA((n,)),
            pltpu.SemaphoreType.DMA((m + 1, 2, SUB)),
            pltpu.SemaphoreType.DMA((m - 1, SUB, 2 * n)),
            pltpu.SemaphoreType.DMA((m, n, SUB)),
            pltpu.SemaphoreType.DMA((2,)),
        ],
        compiler_params=pltpu.CompilerParams(
            collective_id=0, has_side_effects=True, vmem_limit_bytes=56 * 1024 * 1024
        ),
    )(queries[0], keys[0], values[0], out_weight)
    return out[None]


def solution(mesh):
    return jax.shard_map(
        functools.partial(per_device, mesh.shape["seq"], mesh.shape["dp"]),
        mesh=mesh,
        in_specs=(P("dp", "seq", None), P("dp", "seq", None), P("dp", "seq", None), P(None, "dp")),
        out_specs=P("dp", "seq", None),
        check_vma=False,
    )
```
